32 devices in a mesh: ctx: 16 (over z, y, core), tp: 2 (over x).
Axes of the slice: x: 2, y: 2, z: 4, core: 2. Of those that a mesh axis runs over, the one named last changes fastest.
Arguments:
- queries: bfloat16 [8192, 8192], P('ctx', 'tp'), may hold values from -8 to 8
- stacked_keys: bfloat16 [8192, 1024], P('ctx', 'tp'), may hold values from -8 to 8
- stacked_values: bfloat16 [8192, 1024], P('ctx', 'tp'), may hold values from -6 to 6
- doc_start: int32 [8192], P('ctx'), may hold values from 0 to 8191, as said below
- out_weight: bfloat16 [8192, 4096], P('tp'), may hold values from -0.0625 to 0.0625
Outputs:
- projected: bfloat16 [8192, 4096], P('ctx', 'tp')
The draws below stay inside these ranges and needn't reach their ends.
Inputs may be any that keep to these rules, and one draw needn't show every extreme that they name: doc_start[t] is the position of the first token of the document holding token t; documents are contiguous runs of 1 to 4096 tokens, one document holds exactly 4096 tokens and does not begin at the first of a device's rows, and the last token forms a document of its own.
All inputs are finite; a program needn't handle non-finite values.
Results may differ from the reference program's by a relative error of at most 0.014.
Values may be sent and summed in bfloat16 or wider, within the bound.
No kernel may reach another device: no remote copies, remote signals or barrier semaphores. Data moves between devices by JAX's collectives and lax.ppermute only.
A program may use at most 128 MiB of HBM per device.

```python
import math
import jax
import jax.numpy as jnp
from jax import lax

QUERY_HEADS = 64
KEY_VALUE_HEADS = 8
HEAD_WIDTH = 128
DOUT = 4096
CONTEXT_ROWS = 512
PACKED_TOKENS = 8192
SPAN = 8
L_MAX = 4096
N_TP = 2


def draw_queries(key, part):
    complete_shape = (PACKED_TOKENS, QUERY_HEADS * HEAD_WIDTH)
    base = 2.5 * jax.random.normal(jax.random.fold_in(key, 21), complete_shape, jnp.float32)
    return jnp.clip(base, -8.0, 8.0).astype(jnp.bfloat16)


def draw_stacked_keys(key, part):
    complete_shape = (PACKED_TOKENS, KEY_VALUE_HEADS * HEAD_WIDTH)
    base = jax.random.normal(jax.random.fold_in(key, 31), complete_shape, jnp.float32)
    return jnp.clip(base, -8.0, 8.0).astype(jnp.bfloat16)


def draw_doc_start(key, part):
    first_key, second_key, third_key, fourth_key = jax.random.split(key, 4)
    free_blocks = (PACKED_TOKENS - L_MAX) // CONTEXT_ROWS
    lead = jax.random.randint(first_key, (), 0, free_blocks - 1) * CONTEXT_ROWS + jax.random.randint(second_key, (), 1, CONTEXT_ROWS)
    limit = 2 * PACKED_TOKENS + 2 * L_MAX

    def bounded_add(left, right):
        return jnp.minimum(left + right, limit)
    lengths_a = jax.random.randint(third_key, (PACKED_TOKENS,), 1, L_MAX + 1)
    lengths_b = jax.random.randint(fourth_key, (PACKED_TOKENS,), 1, L_MAX + 1)
    ends_a = lax.associative_scan(bounded_add, lengths_a)
    ends_b = lax.associative_scan(bounded_add, lengths_b)
    starts_a = jnp.concatenate([jnp.zeros((1,), jnp.int32), ends_a[:-1].astype(jnp.int32)])
    starts_b = lead + L_MAX + jnp.concatenate([jnp.zeros((1,), jnp.int32), ends_b[:-1].astype(jnp.int32)])
    places = jnp.arange(PACKED_TOKENS, dtype=jnp.int32)
    index_a = jnp.searchsorted(starts_a, places, side='right') - 1
    index_b = jnp.maximum(jnp.searchsorted(starts_b, places, side='right') - 1, 0)
    first_a = starts_a[index_a]
    first_b = starts_b[index_b]
    result = jnp.where(places < lead, first_a, jnp.where(places < lead + L_MAX, lead, first_b))
    result = jnp.where(places == PACKED_TOKENS - 1, PACKED_TOKENS - 1, result)
    return result.astype(jnp.int32)


def shard_levels(own_key, shape, cuts, least, largest):
    level, own = 1.0, jax.random.fold_in(own_key, 6)
    for position, blocks in cuts:
        steps = jnp.exp(jax.random.uniform(jax.random.fold_in(own, position), (blocks,), jnp.float32, least / len(cuts), largest / len(cuts)))
        level = level * jnp.repeat(steps, shape[position] // blocks).reshape([-1 if axis == position else 1 for axis in range(len(shape))])
    return level


def centred(stream_key, extent, deviation, most, cuts=(), kind=jnp.bfloat16):
    array = deviation * jax.random.normal(stream_key, extent, jnp.float32)
    if cuts:
        array = array * shard_levels(stream_key, extent, cuts, -0.22, 0.18)
    return jnp.clip(array, -most, most).astype(kind)


def setup_inputs(seed: int = 0) -> dict:
    keys = jax.random.split(jax.random.key(seed), 6)
    queries = draw_queries(jax.random.fold_in(keys[5], 71), 0)
    stacked_keys = draw_stacked_keys(jax.random.fold_in(keys[5], 71), 0)
    stacked_values = centred(keys[2], (PACKED_TOKENS, KEY_VALUE_HEADS * HEAD_WIDTH), 1.0, 6.0, ((0, 16), (1, 2)))
    doc_start = draw_doc_start(jax.random.fold_in(keys[5], 71), 0)
    out_weight = centred(keys[4], (QUERY_HEADS * HEAD_WIDTH, DOUT), (QUERY_HEADS * HEAD_WIDTH) ** -0.5, 0.0625, ((0, 2),))
    return dict(queries=queries, stacked_keys=stacked_keys, stacked_values=stacked_values, doc_start=doc_start, out_weight=out_weight)


def reference(queries, stacked_keys, stacked_values, doc_start, out_weight):
    queries_per_group = QUERY_HEADS // KEY_VALUE_HEADS
    padding_rows = SPAN * CONTEXT_ROWS
    window_span = padding_rows + CONTEXT_ROWS
    score_scale = 1.0 / math.sqrt(HEAD_WIDTH)
    keys_with_padding = jnp.concatenate([jnp.zeros((padding_rows, KEY_VALUE_HEADS * HEAD_WIDTH), stacked_keys.dtype), stacked_keys], 0)
    values_with_padding = jnp.concatenate([jnp.zeros((padding_rows, KEY_VALUE_HEADS * HEAD_WIDTH), stacked_values.dtype), stacked_values], 0)

    def one_block(block_index):
        first_row = (block_index * CONTEXT_ROWS).astype(jnp.int32)
        query_tile = lax.dynamic_slice_in_dim(queries, first_row, CONTEXT_ROWS, 0).astype(jnp.float32)
        query_tile = query_tile.reshape(CONTEXT_ROWS, KEY_VALUE_HEADS, queries_per_group, HEAD_WIDTH)
        key_tile = lax.dynamic_slice_in_dim(keys_with_padding, first_row, window_span, 0).astype(jnp.float32)
        key_tile = key_tile.reshape(window_span, KEY_VALUE_HEADS, HEAD_WIDTH)
        value_tile = lax.dynamic_slice_in_dim(values_with_padding, first_row, window_span, 0).astype(jnp.float32)
        value_tile = value_tile.reshape(window_span, KEY_VALUE_HEADS, HEAD_WIDTH)
        starts = lax.dynamic_slice_in_dim(doc_start, first_row, CONTEXT_ROWS, 0)
        query_pos = first_row + jnp.arange(CONTEXT_ROWS, dtype=jnp.int32)
        key_pos = first_row - padding_rows + jnp.arange(window_span, dtype=jnp.int32)
        visible = (key_pos[None, :] >= starts[:, None]) & (key_pos[None, :] <= query_pos[:, None])

        def single_head(kv_head):
            query_head = lax.dynamic_index_in_dim(query_tile, kv_head, 1, keepdims=False)
            key_head = lax.dynamic_index_in_dim(key_tile, kv_head, 1, keepdims=False)
            value_head = lax.dynamic_index_in_dim(value_tile, kv_head, 1, keepdims=False)
            scores = jnp.einsum('qgd,kd->gqk', query_head, key_head) * score_scale
            scores = jnp.where(visible[None], scores, -jnp.inf)
            row_max = lax.optimization_barrier(jnp.max(scores, axis=-1, keepdims=True))
            weights = jnp.where(visible[None], jnp.exp(scores - row_max), 0.0)
            rounded = lax.optimization_barrier(weights.astype(jnp.bfloat16)).astype(jnp.float32)
            weighted_sum = jnp.einsum('gqk,kd->gqd', rounded, value_head)
            return (weighted_sum / lax.optimization_barrier(jnp.sum(weights, axis=-1, keepdims=True))).astype(jnp.bfloat16)
        head_outputs = lax.map(single_head, jnp.arange(KEY_VALUE_HEADS, dtype=jnp.int32))
        return head_outputs.transpose(2, 0, 1, 3).reshape(CONTEXT_ROWS, QUERY_HEADS * HEAD_WIDTH)
    attended = lax.map(one_block, jnp.arange(PACKED_TOKENS // CONTEXT_ROWS, dtype=jnp.int32)).reshape(PACKED_TOKENS, QUERY_HEADS * HEAD_WIDTH)
    head_cols = QUERY_HEADS * HEAD_WIDTH // N_TP

    def add_group(index, summed):
        first_col = (index * head_cols).astype(jnp.int32)
        columns = lax.dynamic_slice_in_dim(attended, first_col, head_cols, 1)
        weight_rows = lax.dynamic_slice_in_dim(out_weight, first_col, head_cols, 0)
        partial_value = jnp.dot(columns, weight_rows, preferred_element_type=jnp.float32)
        return summed + lax.optimization_barrier(partial_value.astype(jnp.bfloat16)).astype(jnp.float32)
    summed = lax.fori_loop(0, N_TP, add_group, jnp.zeros((PACKED_TOKENS, DOUT), jnp.float32))
    return summed.astype(jnp.bfloat16)
```

```python
import functools
import math

import jax
import jax.numpy as jnp
from jax import lax
from jax.experimental import pallas as pl
from jax.experimental.pallas import tpu as pltpu
from jax.sharding import PartitionSpec as P

D = 128
GROUP = 8
WIDTH = GROUP * D
UNIT = 512
SCALE = math.log2(math.e) / math.sqrt(D)
SAFE = 4800.0
FLOOR = -1e30
NT = (((1,), (1,)), ((), ()))
F32 = jnp.float32
BF16 = jnp.bfloat16


def params(mib=40):
    return pltpu.CompilerParams(vmem_limit_bytes=mib * 2**20)


def pack_body(me_ref, *refs):
    count = len(refs) // 3
    for i in range(count):
        k_ref, v_ref, out_ref = refs[2 * i], refs[2 * i + 1], refs[2 * count + i]
        out_ref[0, 0] = k_ref[...]
        for j in range(k_ref.shape[0] // D):
            out_ref[0, 1, j * D : (j + 1) * D, :] = v_ref[j * D : (j + 1) * D, :].T


def pack(me, keys, values, held, split):
    rows = keys.shape[0]
    picks = [lambda g, me: (0, g + lax.rem(me[0], 2) * held if split else g)]
    if split:
        picks.append(lambda g, me: (0, g + (1 - lax.rem(me[0], 2)) * held))
    return pl.pallas_call(
        pack_body,
        grid_spec=pltpu.PrefetchScalarGridSpec(
            num_scalar_prefetch=1,
            grid=(held,),
            in_specs=[pl.BlockSpec((rows, D), pick) for pick in picks for _ in range(2)],
            out_specs=[pl.BlockSpec((1, 2, rows, D), lambda g, me: (g, 0, 0, 0))] * len(picks),
        ),
        out_shape=[jax.ShapeDtypeStruct((held, 2, rows, D), BF16)] * len(picks),
        compiler_params=params(),
        name="pack",
    )(me, *[keys, values] * len(picks))


def largest_norm(x):
    squares = (x.astype(F32) * x.astype(F32)).astype(BF16)
    return jnp.max(jnp.dot(squares, jnp.ones((D, D), BF16), preferred_element_type=F32))


def norms_body(me_ref, *refs):
    for side, q_ref in enumerate(refs[:-1]):
        largest = largest_norm(q_ref[:, :D])
        for h in range(1, GROUP):
            largest = jnp.maximum(largest, largest_norm(q_ref[:, h * D : (h + 1) * D]))
        refs[-1][pl.program_id(0) * (len(refs) - 1) + side] = largest


def norms(me, queries, first_head, held):
    rows = queries[0].shape[0]
    return pl.pallas_call(
        norms_body,
        grid_spec=pltpu.PrefetchScalarGridSpec(
            num_scalar_prefetch=1,
            grid=(held,),
            in_specs=[pl.BlockSpec((rows, WIDTH), lambda h, me: (0, first_head(me) + h))]
            * len(queries),
            out_specs=pl.BlockSpec(memory_space=pltpu.SMEM),
        ),
        out_shape=jax.ShapeDtypeStruct((held * len(queries),), F32),
        compiler_params=params(),
        name="norms",
    )(me, *queries)


def attend_body(
    me_ref, *refs, head, slots, sides, group, rows, tile, row, distance, first, last
):
    doc_values, refs = refs[:sides], refs[sides:]
    kv, refs = refs[:slots], refs[slots:]
    docs, refs = refs[:sides], refs[sides:]
    q_refs, q_norms, refs = refs[: len(group)], refs[len(group)], refs[len(group) + 1 :]
    if not first:
        old_acc, old_stat, old_flag, refs = refs[0], refs[1], refs[2], refs[3:]
    if last:
        outs, refs = refs[: len(group)], refs[len(group) :]
        acc, stat, refs = refs[0], refs[1], refs[2:]
    else:
        acc, stat, new_flag, refs = refs[0].at[0], refs[1].at[0], refs[2], refs[3:]
    keys, values, peak, mask, norm, held_q = refs
    me = me_ref[0]
    core = lax.rem(me, 2)
    chip = lax.div(me, 2)
    span = 2 * rows
    stack = UNIT // tile
    units = GROUP // stack
    side = group[0] + pl.program_id(0)

    @pl.when(pl.program_id(0) == 0)
    def _():
        largest = jnp.float32(0)
        for s in range(slots):
            block = kv[s][0].reshape(span, D)
            keys[s * span : (s + 1) * span, :] = block
            largest = jnp.maximum(largest, largest_norm(block))
            for b in range(2):
                for j in range(0, rows, D):
                    at = s * span + b * rows + j
                    values[:, at : at + D] = kv[s][1, b, j : j + D, :]
        norm[0] = largest

    if len(group) == 1:
        q_ref = q_refs[0]
    else:
        q_ref = held_q
        for k in range(len(group)):

            @pl.when(side == group[k])
            def _():
                q_ref[...] = q_refs[k][...]

    def of_side(pieces):
        return pieces[0] if sides == 1 else jnp.where(side == 0, pieces[0], pieces[1])

    part = jnp.where(side == 0, core, 1 - core)
    top = (2 * chip + part) * rows + row
    lowest = of_side([doc[row] for doc in doc_values])
    highest = of_side([doc[row + tile - 1] for doc in doc_values])
    begin = of_side([doc[...] for doc in docs])
    begin = jnp.concatenate([begin] * stack, axis=1)
    place = lax.broadcasted_iota(jnp.int32, (1, UNIT), 1)
    place = top + (lax.rem(place, tile) if stack > 1 else place)

    if first:
        acc[...] = jnp.zeros_like(acc)
        stat[...] = jnp.zeros_like(stat)
    else:
        acc[...] = old_acc[0]
        stat[...] = old_stat[0]
    plain = norm[0] * q_norms[head * sides + side] / D <= SAFE
    if not first:
        plain = plain & (old_flag[side] == 0)
    if not last:
        new_flag[side] = jnp.where(plain, 0, 1)

    def attend_side(q_ref):
        def scores(at, count, u):
            block = keys[pl.ds(at, count), :]
            q = [q_ref[:, pl.ds((u * stack + i) * D, D)] for i in range(stack)]
            q = q[0] if stack == 1 else jnp.concatenate(q, axis=0)
            return lax.dot_general(block, q, NT, preferred_element_type=F32)

        def add(at, count, u, weights):
            stat[u, :8] += jnp.sum(weights.reshape(count // 8, 8, UNIT), axis=0)
            block = values[:, pl.ds(at, count)]
            acc[u] += jnp.dot(block, weights.astype(BF16), preferred_element_type=F32)

        def run(at, count, masked):
            now = scores(at, count, 0)
            for u in range(units):
                later = scores(at, count, u + 1) if u + 1 < units else None
                weights = jnp.exp2(now * SCALE)
                if masked:
                    weights = weights * mask[...]
                add(at, count, u, weights)
                now = later

        def run_shifted(at):
            def unit(u, _):
                visible = mask[...] > 0.0
                now = jnp.where(visible, scores(at, rows, u) * SCALE, FLOOR)
                old = peak[u]
                new = jnp.maximum(old, jnp.max(now, axis=0, keepdims=True))
                fade = jnp.exp2(old - new)
                peak[u] = new
                stat[u, :8] = stat[u, :8] * fade
                acc[u] = acc[u] * fade
                add(at, rows, u, jnp.where(visible, jnp.exp2(now - new), 0.0))
                return 0

            lax.fori_loop(0, units, unit, 0)

        def start_of(s):
            far = jnp.int32(distance(0, me))
            for k in range(1, slots):
                far = jnp.where(s == k, distance(k, me), far)
            return (chip - far) * span

        def is_whole(start):
            return (start >= highest) & (start + span <= top + 1)

        def edges(skip_whole, body):
            def block(n, _):
                start = start_of(lax.div(n, 2))
                key_start = start + jnp.where(lax.rem(n, 2) == 0, core, 1 - core) * rows
                needed = (key_start + rows > lowest) & (key_start < top + tile)
                if skip_whole:
                    needed = needed & jnp.logical_not(is_whole(start))

                @pl.when(needed)
                def _():
                    position = key_start + lax.broadcasted_iota(jnp.int32, (rows, UNIT), 0)
                    mask[...] = ((position >= begin) & (position <= place)).astype(F32)
                    body(pl.multiple_of(n * rows, rows))

                return 0

            lax.fori_loop(0, 2 * slots, block, 0)

        @pl.when(plain)
        def _():
            def whole_slot(s, _):
                @pl.when(is_whole(start_of(s)))
                def _():
                    run(pl.multiple_of(s * span, span), span, False)

                return 0

            lax.fori_loop(0, slots, whole_slot, 0)
            edges(True, lambda at: run(at, rows, True))

        @pl.when(jnp.logical_not(plain))
        def _():
            for u in range(units):
                some = jnp.sum(stat[u, :8], axis=0, keepdims=True) > 0.0
                peak[u] = jnp.where(some, stat[u, 8:9], FLOOR)
            edges(False, run_shifted)
            for u in range(units):
                stat[u, 8:] = jnp.broadcast_to(peak[u], (8, UNIT))

    attend_side(q_ref)

    if last:
        for k in range(len(group)):

            @pl.when(side == group[k])
            def _():
                for u in range(units):
                    inverse = 1.0 / jnp.sum(stat[u, :8], axis=0, keepdims=True)
                    mean = (acc[u] * inverse).astype(BF16).T
                    for i in range(stack):
                        h = u * stack + i
                        outs[k][:, h * D : (h + 1) * D] = mean[i * tile : (i + 1) * tile]


def attend(me, doc_values, kv, distance, docs, queries, first_head, q_norms, head, group, state, last, tile, row):
    slots, sides = len(kv), len(docs)
    rows = docs[0].shape[1]
    first = state is None
    units = GROUP * tile // UNIT
    acc_shape = (units, D, UNIT)
    stat_shape = (units, 16, UNIT)
    in_smem = pl.BlockSpec(memory_space=pltpu.SMEM)
    state_specs = [
        pl.BlockSpec((1,) + shape, lambda i, *s: (group[0] + i, 0, 0, 0)) for shape in (acc_shape, stat_shape)
    ] + [in_smem]
    if last:
        out_specs = [pl.BlockSpec((tile, WIDTH), lambda i, *s: (0, 0))] * len(group)
        out_shape = [jax.ShapeDtypeStruct((tile, WIDTH), BF16)] * len(group)
        held = [pltpu.VMEM(acc_shape, F32), pltpu.VMEM(stat_shape, F32)]
    else:
        out_specs = state_specs
        out_shape = [
            jax.ShapeDtypeStruct((sides,) + shape, F32) for shape in (acc_shape, stat_shape)
        ] + [jax.ShapeDtypeStruct((sides,), jnp.int32)]
        held = []
    work = len(group) * GROUP * tile * slots * 2 * rows
    return pl.pallas_call(
        functools.partial(
            attend_body,
            head=head,
            slots=slots,
            sides=sides,
            group=group,
            rows=rows,
            tile=tile,
            row=row,
            distance=distance,
            first=first,
            last=last,
        ),
        grid_spec=pltpu.PrefetchScalarGridSpec(
            num_scalar_prefetch=1 + sides,
            grid=(len(group),),
            in_specs=[pl.BlockSpec(kv[0].shape, lambda i, *s: (0, 0, 0, 0))] * slots
            + [pl.BlockSpec((1, tile), lambda i, *s: (0, row // tile))] * sides
            + [pl.BlockSpec((tile, WIDTH), lambda i, *s: (row // tile, first_head(s[0]) + head))]
            * len(group)
            + [in_smem]
            + ([] if first else state_specs),
            out_specs=out_specs,
            scratch_shapes=held
            + [
                pltpu.VMEM((slots * 2 * rows, D), BF16),
                pltpu.VMEM((D, slots * 2 * rows), BF16),
                pltpu.VMEM((units, 1, UNIT), F32),
                pltpu.VMEM((rows, UNIT), F32),
                pltpu.SMEM((1,), F32),
                pltpu.VMEM((tile, WIDTH), BF16),
            ],
        ),
        out_shape=out_shape,
        compiler_params=params(),
        cost_estimate=pl.CostEstimate(
            flops=work * D * 6, bytes_accessed=8 * 2**20, transcendentals=work
        ),
        name="attend",
    )(me, *doc_values, *kv, *docs, *[queries[k] for k in group], q_norms, *([] if first else state))


def project_body(me_ref, *refs, blocks):
    count = len(blocks)
    w_ref, out_ref = refs[count], refs[count + 1]
    total = None
    for a, block in zip(refs[:count], blocks):
        at = pl.multiple_of(block(me_ref) * WIDTH, WIDTH)
        term = jnp.dot(a[...], w_ref[pl.ds(at, WIDTH), :], preferred_element_type=F32)
        total = term if total is None else total + term
    out_ref[...] = total.astype(BF16)


def project(me, parts, rows, weight, column, cols):
    tile = min(cols, 256)
    depth = weight.shape[0]
    return pl.pallas_call(
        functools.partial(project_body, blocks=[block for _, _, block in parts]),
        grid_spec=pltpu.PrefetchScalarGridSpec(
            num_scalar_prefetch=1,
            grid=(cols // tile,),
            in_specs=[
                pl.BlockSpec((rows, WIDTH), lambda n, me, at=at: (at, 0)) for _, at, _ in parts
            ]
            + [pl.BlockSpec((depth, tile), lambda n, me: (0, column(me) // tile + n))],
            out_specs=pl.BlockSpec((rows, tile), lambda n, me: (0, n)),
        ),
        out_shape=jax.ShapeDtypeStruct((rows, cols), BF16),
        compiler_params=params(32),
        cost_estimate=pl.CostEstimate(
            flops=2 * rows * cols * depth, bytes_accessed=2 * cols * depth, transcendentals=0
        ),
        name="project",
    )(me, *[a for a, _, _ in parts], weight)


def local(queries, stacked_keys, stacked_values, doc_start, out_weight):
    rows = queries.shape[0]
    heads = stacked_keys.shape[1] // D
    ctx = lax.axis_size("ctx")
    tp = lax.axis_size("tp")
    levels = ctx // 2 // 4
    index = lax.axis_index("ctx")
    me = jnp.stack([index, lax.axis_index("tp")]).astype(jnp.int32)
    is_y0 = lax.rem(lax.div(index, 2), 2) == 0
    split = heads % 2 == 0
    held = heads // 2 if split else heads

    def permuted(x, target):
        return lax.ppermute(x, "ctx", [(i, target(i)) for i in range(ctx)])

    def other_core(x):
        return permuted(x, lambda i: i ^ 1)

    def other_y(x):
        return permuted(x, lambda i: i ^ 2)

    def next_z(x):
        return permuted(x, lambda i: (i + 4) % ctx)

    def after(x, *others):
        return lax.optimization_barrier((x,) + others)[0]

    packed = pack(me, stacked_keys, stacked_values, held, split)
    mine = packed[0]
    theirs = other_core(packed[-1])
    doc_values, docs = [doc_start], [doc_start.reshape(1, rows)]
    owns = [jnp.stack([mine[h], theirs[h]], axis=1) for h in range(held)]
    queries = [queries]

    def first_head(me):
        return lax.rem(me[0], 2) * held if split else 0

    if split:
        doc_values.append(other_core(after(doc_start, owns[0])))
        docs.append(doc_values[1].reshape(1, rows))
        queries.append(other_core(after(queries[0], owns[0])))
    q_norms = norms(me, queries, first_head, held)

    def along_distance(level):
        return lambda me: 2 * level

    def across_distance(level):
        if level < levels:
            return lambda me: 2 * level + 2 * lax.rem(lax.div(me, 2), 2) - 1
        return lambda me: jnp.where(lax.rem(lax.div(me, 2), 2) == 0, 2 * levels - 1, 1)

    sides = tuple(range(len(docs)))

    def call(slots, head, group, state, last, tile=rows, row=0):
        return attend(
            me,
            doc_values,
            [x for x, _ in slots],
            lambda s, me: slots[s][1](me),
            docs,
            queries,
            first_head,
            q_norms,
            head,
            group,
            state,
            last,
            tile,
            row,
        )

    def label(far):
        distances = [along_distance(level) for level in range(2, levels + 1)]
        distances += [across_distance(level) for level in range(1, levels + 1)]
        return list(zip(far, distances))

    def mine_rows(h):
        return lambda me: h + lax.rem(me[0], 2) * held if split else h

    def their_rows(h):
        return lambda me: h + (1 - lax.rem(me[0], 2)) * held

    parts = []

    def finish(got, h):
        parts.append((got[0], 0, mine_rows(h)))
        if split:
            parts.append((other_core(got[1]), 0, their_rows(h)))

    for h in range(held):
        own = owns[h] if h == 0 else after(owns[h], along[-1])
        along = [own, next_z(own)]
        if h == 0:
            along[1], q_norms = lax.optimization_barrier((along[1], q_norms))
        else:
            along[1], far = lax.optimization_barrier((along[1], far))
        across = []
        for level in range(1, levels):
            along.append(next_z(along[level]))
            across.append(other_y(along[level]))
            if level == 1 and h == 0 and held > 1:
                near = [(own, along_distance(0)), (along[1], along_distance(1))]
                state = call(near, h, sides, None, False)
                along[2], across[0], state = lax.optimization_barrier(
                    (along[2], across[0], state)
                )
            if level == 1 and h > 0:
                got = [call(label(far), h - 1, (k,), state, True)[0] for k in sides[1:]]
                along[2], across[0], got = lax.optimization_barrier((along[2], across[0], got))
        across.append(other_y(jnp.where(is_y0, own, along[-1])))
        if h > 0:
            got = [call(label(far), h - 1, sides[:1], state, True)[0]] + got
            across[-1], got = lax.optimization_barrier((across[-1], got))
            finish(got, h - 1)
        near = [(own, along_distance(0)), (along[1], along_distance(1))]
        far = along[2:] + across
        if h > 0 and h + 1 < held:
            state = call(near, h, sides, None, False)
    finish(call(near + label(far), held - 1, sides, None, True), held - 1)

    cols = out_weight.shape[1] // tp
    if tp != 2:
        whole = project(me, parts, rows, out_weight, lambda me: 0, cols * tp)
        return lax.psum_scatter(whole, "tp", scatter_dimension=1, tiled=True)
    chunks = 4
    width = cols // chunks
    away, here = [], []
    for c in range(chunks):
        sent = project(
            me, parts, rows, out_weight, lambda me: (1 - me[1]) * cols + c * width, width
        )
        away.append(lax.ppermute(sent, "tp", [(0, 1), (1, 0)]))
    for c in range(chunks):
        here.append(
            project(me, parts, rows, out_weight, lambda me: me[1] * cols + c * width, width)
        )
    return jnp.concatenate(
        [(a.astype(F32) + b.astype(F32)).astype(BF16) for a, b in zip(here, away)], axis=1
    )


def solution(mesh):
    return jax.shard_map(
        local,
        mesh=mesh,
        in_specs=(P("ctx", "tp"), P("ctx", "tp"), P("ctx", "tp"), P("ctx"), P("tp", None)),
        out_specs=P("ctx", "tp"),
        check_vma=False,
    )
```

```python
import functools
import math

import jax
import jax.numpy as jnp
from jax import lax
from jax.experimental import pallas as pl
from jax.experimental.pallas import tpu as pltpu
from jax.sharding import PartitionSpec as P

D = 128
GROUP = 8
WIDTH = GROUP * D
LIMIT = 22
UNIT = 512
SCALE = math.log2(math.e) / math.sqrt(D)
SAFE = 4800.0
FLOOR = -1e30
NT = (((1,), (1,)), ((), ()))
F32 = jnp.float32
BF16 = jnp.bfloat16


def params(mib=40):
    return pltpu.CompilerParams(vmem_limit_bytes=mib * 2**20)


def pack_body(me_ref, *refs):
    count = len(refs) // 3
    for i in range(count):
        k_ref, v_ref, out_ref = refs[2 * i], refs[2 * i + 1], refs[2 * count + i]
        out_ref[0, 0] = k_ref[...]
        for j in range(k_ref.shape[0] // D):
            out_ref[0, 1, j * D : (j + 1) * D, :] = v_ref[j * D : (j + 1) * D, :].T


def pack(me, keys, values, held, split):
    rows = keys.shape[0]
    picks = [lambda g, me: (0, g + lax.rem(me[0], 2) * held if split else g)]
    if split:
        picks.append(lambda g, me: (0, g + (1 - lax.rem(me[0], 2)) * held))
    return pl.pallas_call(
        pack_body,
        grid_spec=pltpu.PrefetchScalarGridSpec(
            num_scalar_prefetch=1,
            grid=(held,),
            in_specs=[pl.BlockSpec((rows, D), pick) for pick in picks for _ in range(2)],
            out_specs=[pl.BlockSpec((1, 2, rows, D), lambda g, me: (g, 0, 0, 0))] * len(picks),
        ),
        out_shape=[jax.ShapeDtypeStruct((held, 2, rows, D), BF16)] * len(picks),
        compiler_params=params(),
        name="pack",
    )(me, *[keys, values] * len(picks))


def largest_norm(x):
    squares = (x.astype(F32) * x.astype(F32)).astype(BF16)
    return jnp.max(jnp.dot(squares, jnp.ones((D, D), BF16), preferred_element_type=F32))


def attend_body(
    me_ref, *refs, slots, sides, group, rows, tile, row, distance, first, last
):
    doc_values, refs = refs[:sides], refs[sides:]
    kv, refs = refs[:slots], refs[slots:]
    docs, refs = refs[:sides], refs[sides:]
    q_refs, refs = refs[: len(group)], refs[len(group) :]
    if not first:
        old_acc, old_stat, old_norm, refs = refs[0], refs[1], refs[2], refs[3:]
    if last:
        outs, refs = refs[: len(group)], refs[len(group) :]
        acc, stat, refs = refs[0], refs[1], refs[2:]
    else:
        acc, stat, new_norm, refs = refs[0].at[0], refs[1].at[0], refs[2], refs[3:]
    keys, values, peak, mask, norm, held_q = refs
    me = me_ref[0]
    core = lax.rem(me, 2)
    chip = lax.div(me, 2)
    span = 2 * rows
    stack = UNIT // tile
    units = GROUP // stack
    side = group[0] + pl.program_id(0)

    @pl.when(pl.program_id(0) == 0)
    def _():
        largest = jnp.float32(0)
        for s in range(slots):
            block = kv[s][0].reshape(span, D)
            keys[s * span : (s + 1) * span, :] = block
            largest = jnp.maximum(largest, largest_norm(block))
            for b in range(2):
                for j in range(0, rows, D):
                    at = s * span + b * rows + j
                    values[:, at : at + D] = kv[s][1, b, j : j + D, :]
        norm[0] = largest

    if len(group) == 1:
        q_ref = q_refs[0]
    else:
        q_ref = held_q
        for k in range(len(group)):

            @pl.when(side == group[k])
            def _():
                q_ref[...] = q_refs[k][...]

    def of_side(pieces):
        return pieces[0] if sides == 1 else jnp.where(side == 0, pieces[0], pieces[1])

    part = jnp.where(side == 0, core, 1 - core)
    top = (2 * chip + part) * rows + row
    lowest = of_side([doc[row] for doc in doc_values])
    begin = of_side([doc[...] for doc in docs])
    reach = jnp.concatenate([jnp.where(begin == lowest, 1.0, 0.0)] * stack, axis=1)
    begin = jnp.concatenate([begin] * stack, axis=1)
    place = lax.broadcasted_iota(jnp.int32, (1, UNIT), 1)
    place = top + (lax.rem(place, tile) if stack > 1 else place)

    if first:
        acc[...] = jnp.zeros_like(acc)
        stat[...] = jnp.zeros_like(stat)
    else:
        acc[...] = old_acc[0]
        stat[...] = old_stat[0]
    if first:
        q_norm = largest_norm(q_ref[:, :D])
        for h in range(1, GROUP):
            q_norm = jnp.maximum(q_norm, largest_norm(q_ref[:, h * D : (h + 1) * D]))
    else:
        q_norm = old_norm[side]
    plain = norm[0] * q_norm / D <= SAFE
    if not last:
        new_norm[side] = jnp.where(plain, q_norm, jnp.inf)

    def attend_side(q_ref):
        def scores(at, count, u):
            block = keys[pl.ds(at, count), :]
            q = [q_ref[:, pl.ds((u * stack + i) * D, D)] for i in range(stack)]
            q = q[0] if stack == 1 else jnp.concatenate(q, axis=0)
            return lax.dot_general(block, q, NT, preferred_element_type=F32)

        def add(at, count, u, weights, scale=None):
            sums = jnp.sum(weights.reshape(count // 8, 8, UNIT), axis=0)
            block = values[:, pl.ds(at, count)]
            mixed = jnp.dot(block, weights.astype(BF16), preferred_element_type=F32)
            stat[u, :8] += sums if scale is None else sums * scale
            acc[u] += mixed if scale is None else mixed * scale

        def run(at, count, masked):
            now = scores(at, count, 0)
            for u in range(units):
                later = scores(at, count, u + 1) if u + 1 < units else None
                weights = jnp.exp2(now * SCALE)
                if masked:
                    weights = weights * mask[...]
                add(at, count, u, weights, None if masked else reach)
                now = later

        def run_shifted(at):
            def unit(u, _):
                visible = mask[...] > 0.0
                now = jnp.where(visible, scores(at, rows, u) * SCALE, FLOOR)
                old = peak[u]
                new = jnp.maximum(old, jnp.max(now, axis=0, keepdims=True))
                fade = jnp.exp2(old - new)
                peak[u] = new
                stat[u, :8] = stat[u, :8] * fade
                acc[u] = acc[u] * fade
                add(at, rows, u, jnp.where(visible, jnp.exp2(now - new), 0.0))
                return 0

            lax.fori_loop(0, units, unit, 0)

        def start_of(s):
            far = jnp.int32(distance(0, me))
            for k in range(1, slots):
                far = jnp.where(s == k, distance(k, me), far)
            return (chip - far) * span

        def is_whole(start):
            return (start >= lowest) & (start + span <= top)

        def edges(skip_whole, body):
            def block(n, _):
                start = start_of(lax.div(n, 2))
                key_start = start + jnp.where(lax.rem(n, 2) == 0, core, 1 - core) * rows
                needed = (key_start + rows > lowest) & (key_start < top + tile)
                if skip_whole:
                    needed = needed & jnp.logical_not(is_whole(start))

                @pl.when(needed)
                def _():
                    position = key_start + lax.broadcasted_iota(jnp.int32, (rows, UNIT), 0)
                    mask[...] = ((position >= begin) & (position <= place)).astype(F32)
                    body(pl.multiple_of(n * rows, rows))

                return 0

            lax.fori_loop(0, 2 * slots, block, 0)

        @pl.when(plain)
        def _():
            def whole_slot(s, _):
                @pl.when(is_whole(start_of(s)))
                def _():
                    run(pl.multiple_of(s * span, span), span, False)

                return 0

            if not first:
                lax.fori_loop(0, slots, whole_slot, 0)
            edges(True, lambda at: run(at, rows, True))

        @pl.when(jnp.logical_not(plain))
        def _():
            for u in range(units):
                some = jnp.sum(stat[u, :8], axis=0, keepdims=True) > 0.0
                peak[u] = jnp.where(some, stat[u, 8:9], FLOOR)
            edges(False, run_shifted)
            for u in range(units):
                stat[u, 8:] = jnp.broadcast_to(peak[u], (8, UNIT))

    attend_side(q_ref)

    if last:
        for k in range(len(group)):

            @pl.when(side == group[k])
            def _():
                for u in range(units):
                    inverse = 1.0 / jnp.sum(stat[u, :8], axis=0, keepdims=True)
                    mean = (acc[u] * inverse).astype(BF16).T
                    for i in range(stack):
                        h = u * stack + i
                        outs[k][:, h * D : (h + 1) * D] = mean[i * tile : (i + 1) * tile]


def attend(me, doc_values, kv, distance, docs, queries, first_head, head, group, state, last, tile, row):
    slots, sides = len(kv), len(docs)
    rows = docs[0].shape[1]
    first = state is None
    units = GROUP * tile // UNIT
    acc_shape = (units, D, UNIT)
    stat_shape = (units, 16, UNIT)
    in_smem = pl.BlockSpec(memory_space=pltpu.SMEM)
    state_specs = [
        pl.BlockSpec((1,) + shape, lambda i, *s: (group[0] + i, 0, 0, 0)) for shape in (acc_shape, stat_shape)
    ] + [in_smem]
    if last:
        out_specs = [pl.BlockSpec((tile, WIDTH), lambda i, *s: (0, 0))] * len(group)
        out_shape = [jax.ShapeDtypeStruct((tile, WIDTH), BF16)] * len(group)
        held = [pltpu.VMEM(acc_shape, F32), pltpu.VMEM(stat_shape, F32)]
    else:
        out_specs = state_specs
        out_shape = [
            jax.ShapeDtypeStruct((sides,) + shape, F32) for shape in (acc_shape, stat_shape)
        ] + [jax.ShapeDtypeStruct((sides,), F32)]
        held = []
    work = len(group) * GROUP * tile * slots * 2 * rows
    return pl.pallas_call(
        functools.partial(
            attend_body,
            slots=slots,
            sides=sides,
            group=group,
            rows=rows,
            tile=tile,
            row=row,
            distance=distance,
            first=first,
            last=last,
        ),
        grid_spec=pltpu.PrefetchScalarGridSpec(
            num_scalar_prefetch=1 + sides,
            grid=(len(group),),
            in_specs=[
                pl.BlockSpec(
                    kv[0].shape, lambda i, *s: (0, 0, 0, 0), pipeline_mode=pl.Buffered(1)
                )
            ]
            * slots
            + [pl.BlockSpec((1, tile), lambda i, *s: (0, row // tile))] * sides
            + [
                pl.BlockSpec(
                    (tile, WIDTH),
                    lambda i, *s: (row // tile, first_head(s[0]) + head),
                    pipeline_mode=pl.Buffered(1),
                )
            ]
            * len(group)
            + ([] if first else state_specs),
            out_specs=out_specs,
            scratch_shapes=held
            + [
                pltpu.VMEM((slots * 2 * rows, D), BF16),
                pltpu.VMEM((D, slots * 2 * rows), BF16),
                pltpu.VMEM((units, 1, UNIT), F32),
                pltpu.VMEM((rows, UNIT), F32),
                pltpu.SMEM((1,), F32),
                pltpu.VMEM((tile, WIDTH), BF16),
            ],
        ),
        out_shape=out_shape,
        compiler_params=params(LIMIT),
        cost_estimate=pl.CostEstimate(
            flops=work * D * 6, bytes_accessed=8 * 2**20, transcendentals=work
        ),
        name="attend",
    )(me, *doc_values, *kv, *docs, *[queries[k] for k in group], *([] if first else state))


def project_body(me_ref, *refs, blocks):
    count = len(blocks)
    w_ref, out_ref = refs[count], refs[count + 1]
    total = None
    for a, block in zip(refs[:count], blocks):
        at = pl.multiple_of(block(me_ref) * WIDTH, WIDTH)
        term = jnp.dot(a[...], w_ref[pl.ds(at, WIDTH), :], preferred_element_type=F32)
        total = term if total is None else total + term
    out_ref[...] = total.astype(BF16)


def project(me, parts, rows, weight, column, cols):
    tile = min(cols, 256)
    depth = weight.shape[0]
    return pl.pallas_call(
        functools.partial(project_body, blocks=[block for _, _, block in parts]),
        grid_spec=pltpu.PrefetchScalarGridSpec(
            num_scalar_prefetch=1,
            grid=(cols // tile,),
            in_specs=[
                pl.BlockSpec((rows, WIDTH), lambda n, me, at=at: (at, 0)) for _, at, _ in parts
            ]
            + [pl.BlockSpec((depth, tile), lambda n, me: (0, column(me) // tile + n))],
            out_specs=pl.BlockSpec((rows, tile), lambda n, me: (0, n)),
        ),
        out_shape=jax.ShapeDtypeStruct((rows, cols), BF16),
        compiler_params=params(32),
        cost_estimate=pl.CostEstimate(
            flops=2 * rows * cols * depth, bytes_accessed=2 * cols * depth, transcendentals=0
        ),
        name="project",
    )(me, *[a for a, _, _ in parts], weight)


def local(queries, stacked_keys, stacked_values, doc_start, out_weight):
    rows = queries.shape[0]
    heads = stacked_keys.shape[1] // D
    ctx = lax.axis_size("ctx")
    tp = lax.axis_size("tp")
    levels = ctx // 2 // 4
    index = lax.axis_index("ctx")
    me = jnp.stack([index, lax.axis_index("tp")]).astype(jnp.int32)
    is_y0 = lax.rem(lax.div(index, 2), 2) == 0
    split = heads % 2 == 0
    held = heads // 2 if split else heads

    def permuted(x, target):
        return lax.ppermute(x, "ctx", [(i, target(i)) for i in range(ctx)])

    def other_core(x):
        return permuted(x, lambda i: i ^ 1)

    def other_y(x):
        return permuted(x, lambda i: i ^ 2)

    def next_z(x):
        return permuted(x, lambda i: (i + 4) % ctx)

    def after(x, *others):
        return lax.optimization_barrier((x,) + others)[0]

    packed = pack(me, stacked_keys, stacked_values, held, split)
    mine = packed[0]
    theirs = other_core(packed[-1])
    doc_values, docs = [doc_start], [doc_start.reshape(1, rows)]
    owns = [jnp.stack([mine[h], theirs[h]], axis=1) for h in range(held)]
    queries = [queries]

    def first_head(me):
        return lax.rem(me[0], 2) * held if split else 0

    if split:
        doc_values.append(other_core(doc_start))
        docs.append(doc_values[1].reshape(1, rows))
        queries.append(other_core(queries[0]))

    def along_distance(level):
        return lambda me: 2 * level

    def across_distance(level):
        if level < levels:
            return lambda me: 2 * level + 2 * lax.rem(lax.div(me, 2), 2) - 1
        return lambda me: jnp.where(lax.rem(lax.div(me, 2), 2) == 0, 2 * levels - 1, 1)

    sides = tuple(range(len(docs)))

    def call(slots, head, group, state, last, tile=rows, row=0):
        return attend(
            me,
            doc_values,
            [x for x, _ in slots],
            lambda s, me: slots[s][1](me),
            docs,
            queries,
            first_head,
            head,
            group,
            state,
            last,
            tile,
            row,
        )

    def label(far):
        distances = [along_distance(level) for level in range(2, levels + 1)]
        distances += [across_distance(level) for level in range(1, levels + 1)]
        return list(zip(far, distances))

    def mine_rows(h):
        return lambda me: h + lax.rem(me[0], 2) * held if split else h

    def their_rows(h):
        return lambda me: h + (1 - lax.rem(me[0], 2)) * held

    parts = []

    def finish(got, h):
        parts.append((got[0], 0, mine_rows(h)))
        if split:
            parts.append((other_core(got[1]), 0, their_rows(h)))

    previous = None
    for h in range(held):
        own = owns[h] if h == 0 else after(owns[h], along[-1])
        along = [own, next_z(own)]
        state = call([(own, along_distance(0))], h, sides, None, False)
        if h == 0:
            along[1], state = lax.optimization_barrier((along[1], state))
        else:
            along[1], far, state = lax.optimization_barrier((along[1], far, state))
        across = []
        for level in range(1, levels):
            along.append(next_z(along[level]))
            across.append(other_y(along[level]))
            if level == 1 and h == 0 and held > 1:
                state = call([(along[1], along_distance(1))], h, sides, state, False)
                along[2], across[0], state = lax.optimization_barrier(
                    (along[2], across[0], state)
                )
            if level == 1 and h > 0:
                got = [call(label(far), h - 1, (k,), previous, True)[0] for k in sides[1:]]
                along[2], across[0], got = lax.optimization_barrier((along[2], across[0], got))
        across.append(other_y(jnp.where(is_y0, own, along[-1])))
        if h > 0:
            got = [call(label(far), h - 1, sides[:1], previous, True)[0]] + got
            across[-1], got = lax.optimization_barrier((across[-1], got))
            finish(got, h - 1)
        far = along[2:] + across
        if h > 0 and h + 1 < held:
            state = call([(along[1], along_distance(1))], h, sides, state, False)
        previous = state
    finish(call([(along[1], along_distance(1))] + label(far), held - 1, sides, state, True), held - 1)

    cols = out_weight.shape[1] // tp
    if tp != 2:
        whole = project(me, parts, rows, out_weight, lambda me: 0, cols * tp)
        return lax.psum_scatter(whole, "tp", scatter_dimension=1, tiled=True)
    eighth = cols // 8
    cuts = [0, eighth, 3 * eighth, 5 * eighth, 7 * eighth, cols]
    spans = list(zip(cuts, cuts[1:]))
    away, here = [], []
    for at, end in spans:
        sent = project(
            me, parts, rows, out_weight, lambda me: (1 - me[1]) * cols + at, end - at
        )
        away.append(lax.ppermute(sent, "tp", [(0, 1), (1, 0)]))
    for at, end in spans:
        here.append(
            project(me, parts, rows, out_weight, lambda me: me[1] * cols + at, end - at)
        )
    return jnp.concatenate(
        [(a.astype(F32) + b.astype(F32)).astype(BF16) for a, b in zip(here, away)], axis=1
    )


def solution(mesh):
    return jax.shard_map(
        local,
        mesh=mesh,
        in_specs=(P("ctx", "tp"), P("ctx", "tp"), P("ctx", "tp"), P("ctx"), P("tp", None)),
        out_specs=P("ctx", "tp"),
        check_vma=False,
    )
```

```python
import functools
import math

import jax
import jax.numpy as jnp
from jax import lax
from jax.experimental import pallas as pl
from jax.experimental.pallas import tpu as pltpu
from jax.sharding import PartitionSpec as P

D = 128
GROUP = 8
WIDTH = GROUP * D
LIMIT = 22
UNIT = 512
SCALE = math.log2(math.e) / math.sqrt(D)
SAFE = 4800.0
FLOOR = -1e30
NT = (((1,), (1,)), ((), ()))
F32 = jnp.float32
BF16 = jnp.bfloat16


def params(mib=40):
    return pltpu.CompilerParams(vmem_limit_bytes=mib * 2**20)


def pack_body(me_ref, *refs):
    count = len(refs) // 3
    for i in range(count):
        k_ref, v_ref, out_ref = refs[2 * i], refs[2 * i + 1], refs[2 * count + i]
        out_ref[0, 0] = k_ref[...]
        for j in range(k_ref.shape[0] // D):
            out_ref[0, 1, j * D : (j + 1) * D, :] = v_ref[j * D : (j + 1) * D, :].T


def pack(me, keys, values, held, split):
    rows = keys.shape[0]
    picks = [lambda g, me: (0, g + lax.rem(me[0], 2) * held if split else g)]
    if split:
        picks.append(lambda g, me: (0, g + (1 - lax.rem(me[0], 2)) * held))
    return pl.pallas_call(
        pack_body,
        grid_spec=pltpu.PrefetchScalarGridSpec(
            num_scalar_prefetch=1,
            grid=(held,),
            in_specs=[pl.BlockSpec((rows, D), pick) for pick in picks for _ in range(2)],
            out_specs=[pl.BlockSpec((1, 2, rows, D), lambda g, me: (g, 0, 0, 0))] * len(picks),
        ),
        out_shape=[jax.ShapeDtypeStruct((held, 2, rows, D), BF16)] * len(picks),
        compiler_params=params(),
        name="pack",
    )(me, *[keys, values] * len(picks))


def largest_norm(x):
    return jnp.max(
        lax.dot_general(jnp.ones((8, D), BF16), x * x, NT, preferred_element_type=F32)
    )


def attend_body(
    me_ref, *refs, slots, sides, group, rows, tile, row, distance, first, last
):
    doc_values, refs = refs[:sides], refs[sides:]
    kv, refs = refs[:slots], refs[slots:]
    docs, refs = refs[:sides], refs[sides:]
    q_refs, refs = refs[: len(group)], refs[len(group) :]
    if not first:
        old_acc, old_stat, old_norm, refs = refs[0], refs[1], refs[2], refs[3:]
    if last:
        outs, refs = refs[: len(group)], refs[len(group) :]
        acc, stat, refs = refs[0], refs[1], refs[2:]
    else:
        new_acc, new_stat, new_norm, refs = refs[0], refs[1], refs[2], refs[3:]
    keys, values, peak, mask, norm, held_q = refs
    me = me_ref[0]
    core = lax.rem(me, 2)
    chip = lax.div(me, 2)
    span = 2 * rows
    stack = UNIT // tile
    units = GROUP // stack
    side = group[0] + pl.program_id(0)

    @pl.when(pl.program_id(0) == 0)
    def _():
        largest = jnp.float32(0)
        for s in range(slots):
            block = kv[s][0].reshape(span, D)
            keys[s * span : (s + 1) * span, :] = block
            largest = jnp.maximum(largest, largest_norm(block))
            for b in range(2):
                for j in range(0, rows, D):
                    at = s * span + b * rows + j
                    values[:, at : at + D] = kv[s][1, b, j : j + D, :]
        norm[0] = largest

    if len(group) == 1:
        q_ref = q_refs[0]
    else:
        q_ref = held_q
        for k in range(len(group)):

            @pl.when(side == group[k])
            def _():
                q_ref[...] = q_refs[k][...]

    def of_side(pieces):
        return pieces[0] if sides == 1 else jnp.where(side == 0, pieces[0], pieces[1])

    part = jnp.where(side == 0, core, 1 - core)
    top = (2 * chip + part) * rows + row
    lowest = of_side([doc[row] for doc in doc_values])
    begin = of_side([doc[...] for doc in docs])
    reach = jnp.concatenate([jnp.where(begin == lowest, 1.0, 0.0)] * stack, axis=1)
    begin = jnp.concatenate([begin] * stack, axis=1)
    place = lax.broadcasted_iota(jnp.int32, (1, UNIT), 1)
    place = top + (lax.rem(place, tile) if stack > 1 else place)

    if not last:
        acc, stat = new_acc.at[side], new_stat.at[side]
    if first:
        acc[...] = jnp.zeros_like(acc)
        stat[...] = jnp.zeros_like(stat)
    elif last:
        acc[...] = old_acc[side]
        stat[...] = old_stat[side]
    if first:
        q_norm = largest_norm(q_ref[:, :D])
        for h in range(1, GROUP):
            q_norm = jnp.maximum(q_norm, largest_norm(q_ref[:, h * D : (h + 1) * D]))
    else:
        q_norm = old_norm[side]
    plain = norm[0] * q_norm / D <= SAFE
    if not last:
        new_norm[side] = jnp.where(plain, q_norm, jnp.inf)

    def attend_side(q_ref):
        def scores(at, count, u):
            block = keys[pl.ds(at, count), :]
            q = [q_ref[:, pl.ds((u * stack + i) * D, D)] for i in range(stack)]
            q = q[0] if stack == 1 else jnp.concatenate(q, axis=0)
            return lax.dot_general(block, q, NT, preferred_element_type=F32)

        def add(at, count, u, weights, scale=None):
            sums = jnp.sum(weights.reshape(count // 8, 8, UNIT), axis=0)
            block = values[:, pl.ds(at, count)]
            mixed = jnp.dot(block, weights.astype(BF16), preferred_element_type=F32)
            stat[u, :8] += sums if scale is None else sums * scale
            acc[u] += mixed if scale is None else mixed * scale

        def run(at, count, masked):
            now = scores(at, count, 0)
            for u in range(units):
                later = scores(at, count, u + 1) if u + 1 < units else None
                weights = jnp.exp2(now * SCALE)
                if masked:
                    weights = weights * mask[...]
                add(at, count, u, weights, None if masked else reach)
                now = later

        def run_shifted(at):
            def unit(u, _):
                visible = mask[...] > 0.0
                now = jnp.where(visible, scores(at, rows, u) * SCALE, FLOOR)
                old = peak[u]
                new = jnp.maximum(old, jnp.max(now, axis=0, keepdims=True))
                fade = jnp.exp2(old - new)
                peak[u] = new
                stat[u, :8] = stat[u, :8] * fade
                acc[u] = acc[u] * fade
                add(at, rows, u, jnp.where(visible, jnp.exp2(now - new), 0.0))
                return 0

            lax.fori_loop(0, units, unit, 0)

        def start_of(s):
            far = jnp.int32(distance(0, me))
            for k in range(1, slots):
                far = jnp.where(s == k, distance(k, me), far)
            return (chip - far) * span

        def is_whole(start):
            return (start >= lowest) & (start + span <= top)

        def edges(skip_whole, body):
            def block(n, _):
                start = start_of(lax.div(n, 2))
                key_start = start + jnp.where(lax.rem(n, 2) == 0, core, 1 - core) * rows
                needed = (key_start + rows > lowest) & (key_start < top + tile)
                if skip_whole:
                    needed = needed & jnp.logical_not(is_whole(start))

                full = (key_start >= lowest) & (key_start + rows <= top)
                if skip_whole:

                    @pl.when(needed & full)
                    def _():
                        run(pl.multiple_of(n * rows, rows), rows, False)

                    needed = needed & jnp.logical_not(full)

                @pl.when(needed)
                def _():
                    position = key_start + lax.broadcasted_iota(jnp.int32, (rows, UNIT), 0)
                    mask[...] = ((position >= begin) & (position <= place)).astype(F32)
                    body(pl.multiple_of(n * rows, rows))

                return 0

            lax.fori_loop(0, 2 * slots, block, 0)

        @pl.when(plain)
        def _():
            def whole_slot(s, _):
                @pl.when(is_whole(start_of(s)))
                def _():
                    run(pl.multiple_of(s * span, span), span, False)

                return 0

            if not first:
                lax.fori_loop(0, slots, whole_slot, 0)
            edges(True, lambda at: run(at, rows, True))

        @pl.when(jnp.logical_not(plain))
        def _():
            for u in range(units):
                some = jnp.sum(stat[u, :8], axis=0, keepdims=True) > 0.0
                peak[u] = jnp.where(some, stat[u, 8:9], FLOOR)
            edges(False, run_shifted)
            for u in range(units):
                stat[u, 8:] = jnp.broadcast_to(peak[u], (8, UNIT))

    attend_side(q_ref)

    if last:
        for k in range(len(group)):

            @pl.when(side == group[k])
            def _():
                for u in range(units):
                    inverse = 1.0 / jnp.sum(stat[u, :8], axis=0, keepdims=True)
                    mean = (acc[u] * inverse).astype(BF16).T
                    for i in range(stack):
                        h = u * stack + i
                        outs[k][:, h * D : (h + 1) * D] = mean[i * tile : (i + 1) * tile]


def attend(me, doc_values, kv, distance, docs, queries, first_head, head, group, state, last, tile, row):
    slots, sides = len(kv), len(docs)
    rows = docs[0].shape[1]
    first = state is None
    units = GROUP * tile // UNIT
    acc_shape = (units, D, UNIT)
    stat_shape = (units, 16, UNIT)
    in_smem = pl.BlockSpec(memory_space=pltpu.SMEM)
    state_specs = [pl.BlockSpec(memory_space=pltpu.VMEM)] * 2 + [in_smem]
    at = 1 + 2 * sides + slots + len(group)
    aliases = {} if first or last else {at: 0, at + 1: 1}
    if last:
        out_specs = [pl.BlockSpec((tile, WIDTH), lambda i, *s: (0, 0))] * len(group)
        out_shape = [jax.ShapeDtypeStruct((tile, WIDTH), BF16)] * len(group)
        held = [pltpu.VMEM(acc_shape, F32), pltpu.VMEM(stat_shape, F32)]
    else:
        out_specs = state_specs
        out_shape = [
            jax.ShapeDtypeStruct((sides,) + shape, F32) for shape in (acc_shape, stat_shape)
        ] + [jax.ShapeDtypeStruct((sides,), F32)]
        held = []
    work = len(group) * GROUP * tile * slots * 2 * rows
    return pl.pallas_call(
        functools.partial(
            attend_body,
            slots=slots,
            sides=sides,
            group=group,
            rows=rows,
            tile=tile,
            row=row,
            distance=distance,
            first=first,
            last=last,
        ),
        grid_spec=pltpu.PrefetchScalarGridSpec(
            num_scalar_prefetch=1 + sides,
            grid=(len(group),),
            in_specs=[
                pl.BlockSpec(
                    kv[0].shape, lambda i, *s: (0, 0, 0, 0), pipeline_mode=pl.Buffered(1)
                )
            ]
            * slots
            + [pl.BlockSpec((1, tile), lambda i, *s: (0, row // tile))] * sides
            + [
                pl.BlockSpec(
                    (tile, WIDTH),
                    lambda i, *s: (row // tile, first_head(s[0]) + head),
                    pipeline_mode=pl.Buffered(1),
                )
            ]
            * len(group)
            + ([] if first else state_specs),
            out_specs=out_specs,
            scratch_shapes=held
            + [
                pltpu.VMEM((slots * 2 * rows, D), BF16),
                pltpu.VMEM((D, slots * 2 * rows), BF16),
                pltpu.VMEM((units, 1, UNIT), F32),
                pltpu.VMEM((rows, UNIT), F32),
                pltpu.SMEM((1,), F32),
                pltpu.VMEM((tile, WIDTH), BF16),
            ],
        ),
        out_shape=out_shape,
        input_output_aliases=aliases,
        compiler_params=params(LIMIT),
        cost_estimate=pl.CostEstimate(
            flops=work * D * 6, bytes_accessed=8 * 2**20, transcendentals=work
        ),
        name="attend",
    )(me, *doc_values, *kv, *docs, *[queries[k] for k in group], *([] if first else state))


def project_body(me_ref, *refs, blocks):
    count = len(blocks)
    w_ref, out_ref = refs[count], refs[count + 1]
    total = None
    for a, block in zip(refs[:count], blocks):
        at = pl.multiple_of(block(me_ref) * WIDTH, WIDTH)
        term = jnp.dot(a[...], w_ref[pl.ds(at, WIDTH), :], preferred_element_type=F32)
        total = term if total is None else total + term
    out_ref[...] = total.astype(BF16)


def project(me, parts, rows, weight, column, cols):
    tile = min(cols, 256)
    depth = weight.shape[0]
    return pl.pallas_call(
        functools.partial(project_body, blocks=[block for _, block in parts]),
        grid_spec=pltpu.PrefetchScalarGridSpec(
            num_scalar_prefetch=1,
            grid=(cols // tile,),
            in_specs=[pl.BlockSpec(memory_space=pltpu.VMEM)] * len(parts)
            + [pl.BlockSpec((depth, tile), lambda n, me: (0, column(me) // tile + n))],
            out_specs=pl.BlockSpec((rows, tile), lambda n, me: (0, n)),
        ),
        out_shape=jax.ShapeDtypeStruct((rows, cols), BF16),
        compiler_params=params(32),
        cost_estimate=pl.CostEstimate(
            flops=2 * rows * cols * depth, bytes_accessed=2 * cols * depth, transcendentals=0
        ),
        name="project",
    )(me, *[a for a, _ in parts], weight)


def local(queries, stacked_keys, stacked_values, doc_start, out_weight):
    rows = queries.shape[0]
    heads = stacked_keys.shape[1] // D
    ctx = lax.axis_size("ctx")
    tp = lax.axis_size("tp")
    levels = ctx // 2 // 4
    index = lax.axis_index("ctx")
    me = jnp.stack([index, lax.axis_index("tp")]).astype(jnp.int32)
    is_y0 = lax.rem(lax.div(index, 2), 2) == 0
    split = heads % 2 == 0
    held = heads // 2 if split else heads

    def permuted(x, target):
        return lax.ppermute(x, "ctx", [(i, target(i)) for i in range(ctx)])

    def other_core(x):
        return permuted(x, lambda i: i ^ 1)

    def other_y(x):
        return permuted(x, lambda i: i ^ 2)

    def next_z(x):
        return permuted(x, lambda i: (i + 4) % ctx)

    def after(x, *others):
        return lax.optimization_barrier((x,) + others)[0]

    packed = pack(me, stacked_keys, stacked_values, held, split)
    mine = packed[0]
    theirs = other_core(packed[-1])
    doc_values, docs = [doc_start], [doc_start.reshape(1, rows)]
    owns = [jnp.stack([mine[h], theirs[h]], axis=1) for h in range(held)]
    queries = [queries]

    def first_head(me):
        return lax.rem(me[0], 2) * held if split else 0

    if split:
        doc_values.append(other_core(doc_start))
        docs.append(doc_values[1].reshape(1, rows))
        queries.append(other_core(queries[0]))

    def along_distance(level):
        return lambda me: 2 * level

    def across_distance(level):
        if level < levels:
            return lambda me: 2 * level + 2 * lax.rem(lax.div(me, 2), 2) - 1
        return lambda me: jnp.where(lax.rem(lax.div(me, 2), 2) == 0, 2 * levels - 1, 1)

    sides = tuple(range(len(docs)))

    def call(slots, head, group, state, last, tile=rows, row=0):
        return attend(
            me,
            doc_values,
            [x for x, _ in slots],
            lambda s, me: slots[s][1](me),
            docs,
            queries,
            first_head,
            head,
            group,
            state,
            last,
            tile,
            row,
        )

    def label(far):
        distances = [along_distance(level) for level in range(2, levels + 1)]
        distances += [across_distance(level) for level in range(1, levels + 1)]
        return list(zip(far, distances))

    def mine_rows(h):
        return lambda me: h + lax.rem(me[0], 2) * held if split else h

    def their_rows(h):
        return lambda me: h + (1 - lax.rem(me[0], 2)) * held

    parts = []

    def finish(got, h):
        parts.append(got[0])
        if split:
            parts.append(other_core(got[1]))

    previous = None
    for h in range(held):
        own = owns[h] if h == 0 else after(owns[h], along[-1])
        along = [own, next_z(own)]
        state = call([(own, along_distance(0))], h, sides, None, False)
        if h == 0:
            along[1], state = lax.optimization_barrier((along[1], state))
        else:
            along[1], far, state = lax.optimization_barrier((along[1], far, state))
        across = []
        for level in range(1, levels):
            along.append(next_z(along[level]))
            across.append(other_y(along[level]))
            if level == 1 and h == 0 and held > 1:
                state = call([(along[1], along_distance(1))], h, sides, state, False)
                along[2], across[0], state = lax.optimization_barrier(
                    (along[2], across[0], state)
                )
            if level == 1 and h > 0:
                got = [call(label(far), h - 1, (k,), previous, True)[0] for k in sides[1:]]
                along[2], across[0], got = lax.optimization_barrier((along[2], across[0], got))
        across.append(other_y(jnp.where(is_y0, own, along[-1])))
        if h > 0:
            got = [call(label(far), h - 1, sides[:1], previous, True)[0]] + got
            finish(got, h - 1)
            across[-1], state, parts = lax.optimization_barrier((across[-1], state, parts))
        far = along[2:] + across
        if h > 0 and h + 1 < held:
            state = call([(along[1], along_distance(1))], h, sides, state, False)
        previous = state
    finish(call([(along[1], along_distance(1))] + label(far), held - 1, sides, state, True), held - 1)

    meets = [rule(h) for h in range(held) for rule in (mine_rows, their_rows)[: len(sides)]]
    parts = list(zip(parts, meets))
    cols = out_weight.shape[1] // tp
    if tp != 2:
        whole = project(me, parts, rows, out_weight, lambda me: 0, cols * tp)
        return lax.psum_scatter(whole, "tp", scatter_dimension=1, tiled=True)
    eighth = cols // 8
    cuts = [0, eighth, 3 * eighth, 5 * eighth, 7 * eighth, cols]
    spans = list(zip(cuts, cuts[1:]))[::-1]
    away, here = [], []
    for at, end in spans:
        sent = project(
            me, parts, rows, out_weight, lambda me: (1 - me[1]) * cols + at, end - at
        )
        away.append(lax.ppermute(sent, "tp", [(0, 1), (1, 0)]))
    for at, end in spans:
        here.append(
            project(me, parts, rows, out_weight, lambda me: me[1] * cols + at, end - at)
        )
    return jnp.concatenate(
        [(a.astype(F32) + b.astype(F32)).astype(BF16) for a, b in zip(here, away)][::-1], axis=1
    )


def solution(mesh):
    return jax.shard_map(
        local,
        mesh=mesh,
        in_specs=(P("ctx", "tp"), P("ctx", "tp"), P("ctx", "tp"), P("ctx"), P("tp", None)),
        out_specs=P("ctx", "tp"),
        check_vma=False,
    )
```

```python
import functools
import math

import jax
import jax.numpy as jnp
from jax import lax
from jax.experimental import pallas as pl
from jax.experimental.pallas import tpu as pltpu
from jax.sharding import PartitionSpec as P

D = 128
GROUP = 8
WIDTH = GROUP * D
LIMIT = 22
UNIT = 512
SCALE = math.log2(math.e) / math.sqrt(D)
SAFE = 4800.0
FLOOR = -1e30
NT = (((1,), (1,)), ((), ()))
F32 = jnp.float32
BF16 = jnp.bfloat16


def params(mib=40):
    return pltpu.CompilerParams(vmem_limit_bytes=mib * 2**20)


def pack_body(me_ref, *refs):
    count = len(refs) // 3
    for i in range(count):
        k_ref, v_ref, out_ref = refs[2 * i], refs[2 * i + 1], refs[2 * count + i]
        out_ref[0, 0] = k_ref[...]
        for j in range(k_ref.shape[0] // D):
            out_ref[0, 1, j * D : (j + 1) * D, :] = v_ref[j * D : (j + 1) * D, :].T


def pack(me, keys, values, held, split):
    rows = keys.shape[0]
    picks = [lambda g, me: (0, g + lax.rem(me[0], 2) * held if split else g)]
    if split:
        picks.append(lambda g, me: (0, g + (1 - lax.rem(me[0], 2)) * held))
    return pl.pallas_call(
        pack_body,
        grid_spec=pltpu.PrefetchScalarGridSpec(
            num_scalar_prefetch=1,
            grid=(held,),
            in_specs=[pl.BlockSpec((rows, D), pick) for pick in picks for _ in range(2)],
            out_specs=[pl.BlockSpec((1, 2, rows, D), lambda g, me: (g, 0, 0, 0))] * len(picks),
        ),
        out_shape=[jax.ShapeDtypeStruct((held, 2, rows, D), BF16)] * len(picks),
        compiler_params=params(),
        name="pack",
    )(me, *[keys, values] * len(picks))


def largest_norm(x):
    return jnp.max(
        lax.dot_general(jnp.ones((8, D), BF16), x * x, NT, preferred_element_type=F32)
    )


def attend_body(
    me_ref, *refs, slots, sides, group, rows, tile, row, distance, first, last
):
    doc_values, refs = refs[:sides], refs[sides:]
    kv, refs = refs[:slots], refs[slots:]
    docs, refs = refs[:sides], refs[sides:]
    q_refs, refs = refs[: len(group)], refs[len(group) :]
    if not first:
        old_acc, old_stat, old_norm, refs = refs[0], refs[1], refs[2], refs[3:]
    if last:
        outs, refs = refs[: len(group)], refs[len(group) :]
        acc, stat, refs = refs[0], refs[1], refs[2:]
    else:
        new_acc, new_stat, new_norm, refs = refs[0], refs[1], refs[2], refs[3:]
    keys, values, peak, mask, norm, held_q = refs
    me = me_ref[0]
    core = lax.rem(me, 2)
    chip = lax.div(me, 2)
    span = 2 * rows
    stack = UNIT // tile
    units = GROUP // stack
    side = group[0] + pl.program_id(0)

    @pl.when(pl.program_id(0) == 0)
    def _():
        largest = jnp.float32(0)
        for s in range(slots):
            block = kv[s][0].reshape(span, D)
            keys[s * span : (s + 1) * span, :] = block
            largest = jnp.maximum(largest, largest_norm(block))
            for b in range(2):
                for j in range(0, rows, D):
                    at = s * span + b * rows + j
                    values[:, at : at + D] = kv[s][1, b, j : j + D, :]
        norm[0] = largest

    if len(group) == 1:
        q_ref = q_refs[0]
    else:
        q_ref = held_q
        for k in range(len(group)):

            @pl.when(side == group[k])
            def _():
                q_ref[...] = q_refs[k][...]

    def of_side(pieces):
        return pieces[0] if sides == 1 else jnp.where(side == 0, pieces[0], pieces[1])

    part = jnp.where(side == 0, core, 1 - core)
    top = (2 * chip + part) * rows + row
    lowest = of_side([doc[row] for doc in doc_values])
    begin = of_side([doc[...] for doc in docs])
    reach = jnp.concatenate([jnp.where(begin == lowest, 1.0, 0.0)] * stack, axis=1)
    begin = jnp.concatenate([begin] * stack, axis=1)
    place = lax.broadcasted_iota(jnp.int32, (1, UNIT), 1)
    place = top + (lax.rem(place, tile) if stack > 1 else place)

    if not last:
        acc, stat = new_acc.at[side], new_stat.at[side]
    if first:
        acc[...] = jnp.zeros_like(acc)
        stat[...] = jnp.zeros_like(stat)
    elif last:
        acc[...] = old_acc[side]
        stat[...] = old_stat[side]
    if first:
        q_norm = largest_norm(q_ref[:, :D])
        for h in range(1, GROUP):
            q_norm = jnp.maximum(q_norm, largest_norm(q_ref[:, h * D : (h + 1) * D]))
    else:
        q_norm = old_norm[side]
    plain = norm[0] * q_norm / D <= SAFE
    if not last:
        new_norm[side] = jnp.where(plain, q_norm, jnp.inf)

    def attend_side(q_ref):
        def scores(at, count, u):
            block = keys[pl.ds(at, count), :]
            q = [q_ref[:, pl.ds((u * stack + i) * D, D)] for i in range(stack)]
            q = q[0] if stack == 1 else jnp.concatenate(q, axis=0)
            return lax.dot_general(block, q, NT, preferred_element_type=F32)

        def add(at, count, u, weights, scale=None):
            sums = jnp.sum(weights.reshape(count // 8, 8, UNIT), axis=0)
            block = values[:, pl.ds(at, count)]
            mixed = jnp.dot(block, weights.astype(BF16), preferred_element_type=F32)
            stat[u, :8] += sums if scale is None else sums * scale
            acc[u] += mixed if scale is None else mixed * scale

        def run(at, count, masked):
            now = scores(at, count, 0)
            for u in range(units):
                later = scores(at, count, u + 1) if u + 1 < units else None
                weights = jnp.exp2(now * SCALE)
                if masked:
                    weights = weights * mask[...]
                add(at, count, u, weights, None if masked else reach)
                now = later

        def run_shifted(at):
            def unit(u, _):
                visible = mask[...] > 0.0
                now = jnp.where(visible, scores(at, rows, u) * SCALE, FLOOR)
                old = peak[u]
                new = jnp.maximum(old, jnp.max(now, axis=0, keepdims=True))
                fade = jnp.exp2(old - new)
                peak[u] = new
                stat[u, :8] = stat[u, :8] * fade
                acc[u] = acc[u] * fade
                add(at, rows, u, jnp.where(visible, jnp.exp2(now - new), 0.0))
                return 0

            lax.fori_loop(0, units, unit, 0)

        def start_of(s):
            far = jnp.int32(distance(0, me))
            for k in range(1, slots):
                far = jnp.where(s == k, distance(k, me), far)
            return (chip - far) * span

        def is_whole(start):
            return (start >= lowest) & (start + span <= top)

        def edges(skip_whole, body):
            def block(n, _):
                start = start_of(lax.div(n, 2))
                key_start = start + jnp.where(lax.rem(n, 2) == 0, core, 1 - core) * rows
                needed = (key_start + rows > lowest) & (key_start < top + tile)
                if skip_whole:
                    needed = needed & jnp.logical_not(is_whole(start))

                full = (key_start >= lowest) & (key_start + rows <= top)
                if skip_whole:

                    @pl.when(needed & full)
                    def _():
                        run(pl.multiple_of(n * rows, rows), rows, False)

                    needed = needed & jnp.logical_not(full)

                @pl.when(needed)
                def _():
                    position = key_start + lax.broadcasted_iota(jnp.int32, (rows, UNIT), 0)
                    mask[...] = ((position >= begin) & (position <= place)).astype(F32)
                    body(pl.multiple_of(n * rows, rows))

                return 0

            lax.fori_loop(0, 2 * slots, block, 0)

        @pl.when(plain)
        def _():
            def whole_slot(s, _):
                @pl.when(is_whole(start_of(s)))
                def _():
                    run(pl.multiple_of(s * span, span), span, False)

                return 0

            if not first:
                lax.fori_loop(0, slots, whole_slot, 0)
            edges(True, lambda at: run(at, rows, True))

        @pl.when(jnp.logical_not(plain))
        def _():
            for u in range(units):
                some = jnp.sum(stat[u, :8], axis=0, keepdims=True) > 0.0
                peak[u] = jnp.where(some, stat[u, 8:9], FLOOR)
            edges(False, run_shifted)
            for u in range(units):
                stat[u, 8:] = jnp.broadcast_to(peak[u], (8, UNIT))

    attend_side(q_ref)

    if last:
        for k in range(len(group)):

            @pl.when(side == group[k])
            def _():
                for u in range(units):
                    inverse = 1.0 / jnp.sum(stat[u, :8], axis=0, keepdims=True)
                    mean = (acc[u] * inverse).astype(BF16).T
                    for i in range(stack):
                        h = u * stack + i
                        outs[k][:, h * D : (h + 1) * D] = mean[i * tile : (i + 1) * tile]


def attend(me, doc_values, kv, distance, docs, queries, first_head, head, group, state, last, tile, row):
    slots, sides = len(kv), len(docs)
    rows = docs[0].shape[1]
    first = state is None
    units = GROUP * tile // UNIT
    acc_shape = (units, D, UNIT)
    stat_shape = (units, 16, UNIT)
    in_smem = pl.BlockSpec(memory_space=pltpu.SMEM)
    state_specs = [pl.BlockSpec(memory_space=pltpu.VMEM)] * 2 + [in_smem]
    at = 1 + 2 * sides + slots + len(group)
    aliases = {} if first or last else {at: 0, at + 1: 1}
    if last:
        out_specs = [pl.BlockSpec((tile, WIDTH), lambda i, *s: (0, 0))] * len(group)
        out_shape = [jax.ShapeDtypeStruct((tile, WIDTH), BF16)] * len(group)
        held = [pltpu.VMEM(acc_shape, F32), pltpu.VMEM(stat_shape, F32)]
    else:
        out_specs = state_specs
        out_shape = [
            jax.ShapeDtypeStruct((sides,) + shape, F32) for shape in (acc_shape, stat_shape)
        ] + [jax.ShapeDtypeStruct((sides,), F32)]
        held = []
    work = len(group) * GROUP * tile * slots * 2 * rows
    return pl.pallas_call(
        functools.partial(
            attend_body,
            slots=slots,
            sides=sides,
            group=group,
            rows=rows,
            tile=tile,
            row=row,
            distance=distance,
            first=first,
            last=last,
        ),
        grid_spec=pltpu.PrefetchScalarGridSpec(
            num_scalar_prefetch=1 + sides,
            grid=(len(group),),
            in_specs=[
                pl.BlockSpec(
                    kv[0].shape, lambda i, *s: (0, 0, 0, 0), pipeline_mode=pl.Buffered(1)
                )
            ]
            * slots
            + [pl.BlockSpec((1, tile), lambda i, *s: (0, row // tile))] * sides
            + [
                pl.BlockSpec(
                    (tile, WIDTH),
                    lambda i, *s: (row // tile, first_head(s[0]) + head),
                    pipeline_mode=pl.Buffered(1),
                )
            ]
            * len(group)
            + ([] if first else state_specs),
            out_specs=out_specs,
            scratch_shapes=held
            + [
                pltpu.VMEM((slots * 2 * rows, D), BF16),
                pltpu.VMEM((D, slots * 2 * rows), BF16),
                pltpu.VMEM((units, 1, UNIT), F32),
                pltpu.VMEM((rows, UNIT), F32),
                pltpu.SMEM((1,), F32),
                pltpu.VMEM((tile, WIDTH), BF16),
            ],
        ),
        out_shape=out_shape,
        input_output_aliases=aliases,
        compiler_params=params(LIMIT),
        cost_estimate=pl.CostEstimate(
            flops=work * D * 6, bytes_accessed=8 * 2**20, transcendentals=work
        ),
        name="attend",
    )(me, *doc_values, *kv, *docs, *[queries[k] for k in group], *([] if first else state))


def project_body(me_ref, *refs, blocks):
    count = len(blocks)
    w_ref, out_ref = refs[count], refs[count + 1]
    total = None
    for a, block in zip(refs[:count], blocks):
        at = pl.multiple_of(block(me_ref) * WIDTH, WIDTH)
        term = jnp.dot(a[...], w_ref[pl.ds(at, WIDTH), :], preferred_element_type=F32)
        total = term if total is None else total + term
    out_ref[...] = total.astype(BF16)


def project(me, parts, rows, weight, column, cols):
    tile = min(cols, 256)
    depth = weight.shape[0]
    return pl.pallas_call(
        functools.partial(project_body, blocks=[block for _, block in parts]),
        grid_spec=pltpu.PrefetchScalarGridSpec(
            num_scalar_prefetch=1,
            grid=(cols // tile,),
            in_specs=[pl.BlockSpec(memory_space=pltpu.VMEM)] * len(parts)
            + [pl.BlockSpec((depth, tile), lambda n, me: (0, column(me) // tile + n))],
            out_specs=pl.BlockSpec((rows, tile), lambda n, me: (0, n)),
        ),
        out_shape=jax.ShapeDtypeStruct((rows, cols), BF16),
        compiler_params=params(32),
        cost_estimate=pl.CostEstimate(
            flops=2 * rows * cols * depth, bytes_accessed=2 * cols * depth, transcendentals=0
        ),
        name="project",
    )(me, *[a for a, _ in parts], weight)


def local(queries, stacked_keys, stacked_values, doc_start, out_weight):
    rows = queries.shape[0]
    heads = stacked_keys.shape[1] // D
    ctx = lax.axis_size("ctx")
    tp = lax.axis_size("tp")
    levels = ctx // 2 // 4
    index = lax.axis_index("ctx")
    me = jnp.stack([index, lax.axis_index("tp")]).astype(jnp.int32)
    is_y0 = lax.rem(lax.div(index, 2), 2) == 0
    split = heads % 2 == 0
    held = heads // 2 if split else heads

    def permuted(x, target):
        return lax.ppermute(x, "ctx", [(i, target(i)) for i in range(ctx)])

    def other_core(x):
        return permuted(x, lambda i: i ^ 1)

    def other_y(x):
        return permuted(x, lambda i: i ^ 2)

    def next_z(x):
        return permuted(x, lambda i: (i + 4) % ctx)

    def after(x, *others):
        return lax.optimization_barrier((x,) + others)[0]

    packed = pack(me, stacked_keys, stacked_values, held, split)
    mine = packed[0]
    theirs = other_core(packed[-1])
    doc_values, docs = [doc_start], [doc_start.reshape(1, rows)]
    owns = [jnp.stack([mine[h], theirs[h]], axis=1) for h in range(held)]
    queries = [queries]

    def first_head(me):
        return lax.rem(me[0], 2) * held if split else 0

    if split:
        doc_values.append(other_core(doc_start))
        docs.append(doc_values[1].reshape(1, rows))
        queries.append(other_core(queries[0]))

    def along_distance(level):
        return lambda me: 2 * level

    def across_distance(level):
        if level < levels:
            return lambda me: 2 * level + 2 * lax.rem(lax.div(me, 2), 2) - 1
        return lambda me: jnp.where(lax.rem(lax.div(me, 2), 2) == 0, 2 * levels - 1, 1)

    sides = tuple(range(len(docs)))

    def call(slots, head, group, state, last, tile=rows, row=0):
        return attend(
            me,
            doc_values,
            [x for x, _ in slots],
            lambda s, me: slots[s][1](me),
            docs,
            queries,
            first_head,
            head,
            group,
            state,
            last,
            tile,
            row,
        )

    def label(far):
        distances = [along_distance(level) for level in range(2, levels + 1)]
        distances += [across_distance(level) for level in range(1, levels + 1)]
        return list(zip(far, distances))

    def mine_rows(h):
        return lambda me: h + lax.rem(me[0], 2) * held if split else h

    def their_rows(h):
        return lambda me: h + (1 - lax.rem(me[0], 2)) * held

    parts = []

    def finish(got, h):
        parts.append(got[0])
        if split:
            parts.append(other_core(got[1]))

    previous = None
    for h in range(held):
        own = owns[h] if h == 0 else after(owns[h], along[-1])
        along = [own, next_z(own)]
        state = call([(own, along_distance(0))], h, sides, None, False)
        if h == 0:
            along[1], state = lax.optimization_barrier((along[1], state))
        else:
            along[1], far, state = lax.optimization_barrier((along[1], far, state))
        across = []
        for level in range(1, levels):
            along.append(next_z(along[level]))
            across.append(other_y(along[level]))
            if level == 1 and h == 0 and held > 1:
                state = call([(along[1], along_distance(1))], h, sides, state, False)
                along[2], across[0], state = lax.optimization_barrier(
                    (along[2], across[0], state)
                )
            if level == 1 and h > 0:
                got = [call(label(far), h - 1, (k,), previous, True)[0] for k in sides[1:]]
                along[2], across[0], got = lax.optimization_barrier((along[2], across[0], got))
        across.append(other_y(jnp.where(is_y0, own, along[-1])))
        if h > 0:
            got = [call(label(far), h - 1, sides[:1], previous, True)[0]] + got
            finish(got, h - 1)
            state = call([(along[1], along_distance(1))], h, sides, state, False)
            across[-1], state, parts = lax.optimization_barrier((across[-1], state, parts))
        far = along[2:] + across
        previous = state
    rest = label(far) if held > 1 else [(along[1], along_distance(1))] + label(far)
    finish(call(rest, held - 1, sides, state, True), held - 1)

    meets = [rule(h) for h in range(held) for rule in (mine_rows, their_rows)[: len(sides)]]
    parts = list(zip(parts, meets))
    cols = out_weight.shape[1] // tp
    if tp != 2:
        whole = project(me, parts, rows, out_weight, lambda me: 0, cols * tp)
        return lax.psum_scatter(whole, "tp", scatter_dimension=1, tiled=True)
    eighth = cols // 8
    cuts = [0, eighth, 3 * eighth, 5 * eighth, 7 * eighth, cols]
    spans = list(zip(cuts, cuts[1:]))[::-1]
    away, here = [], []
    for at, end in spans:
        sent = project(
            me, parts, rows, out_weight, lambda me: (1 - me[1]) * cols + at, end - at
        )
        away.append(lax.ppermute(sent, "tp", [(0, 1), (1, 0)]))
    for at, end in spans:
        here.append(
            project(me, parts, rows, out_weight, lambda me: me[1] * cols + at, end - at)
        )
    return jnp.concatenate(
        [(a.astype(F32) + b.astype(F32)).astype(BF16) for a, b in zip(here, away)][::-1], axis=1
    )


def solution(mesh):
    return jax.shard_map(
        local,
        mesh=mesh,
        in_specs=(P("ctx", "tp"), P("ctx", "tp"), P("ctx", "tp"), P("ctx"), P("tp", None)),
        out_specs=P("ctx", "tp"),
        check_vma=False,
    )
```
